256 devices in a mesh: query: 16 (over x_hi, z), feat: 16 (over x_lo, y, core).
Axes of the slice: x: 4 (x_hi: 2, x_lo: 2; x = x_hi * 2 + x_lo), y: 4, z: 8, core: 2. Of those that a mesh axis runs over, the one named last changes fastest.
Arguments:
- query_grads: bfloat16 [8192, 65536], P('query', 'feat'), may hold values from -6 to 6
- train_grads: bfloat16 [2048, 65536], P('query', 'feat'), may hold values from -0.03125 to 0.03125
- eigenvalues: float32 [65536], P('feat'), may hold values from 0.05 to 5
- offsets: int32 [33], replicated, may hold values from 0 to 65536, as said below
Outputs:
- scores: float32 [2048, 8192], P('feat', 'query')
The draws below stay inside these ranges and needn't reach their ends.
Inputs may be any that keep to these rules, and one draw needn't show every extreme that they name: offsets[0] = 0, offsets[32] = 65536, strictly increasing; each block holds between 1536 and 2560 features.
All inputs are finite; a program needn't handle non-finite values.
Results may differ from the reference program's by a relative error of at most 0.0029.
Values may be sent and summed in bfloat16 or wider, within the bound.
A program may use at most 64 MiB of HBM per device.

```python
import math
import jax
import jax.numpy as jnp
from jax import lax

F = 65536
LAYERS = 32
NQ = 8192
NT = 2048


def draw_offsets(key, part):
    key = jax.random.fold_in(key, 7)
    half = LAYERS // 2
    spread = F // (4 * LAYERS)
    deltas = jax.random.randint(key, (half,), -spread, spread + 1, dtype=jnp.int32)
    paired = jnp.stack([deltas, -deltas], axis=1).reshape(LAYERS)
    blocks = F // LAYERS + paired
    return jnp.concatenate([jnp.zeros((1,), jnp.int32), jnp.cumsum(blocks).astype(jnp.int32)])


def raised(values, stream_key, source, target, shards_of, factor):
    owner, partner = [(jnp.arange(values.shape[position]) // (values.shape[position] // shards_of)).reshape([-1 if axis == position else 1 for axis in range(values.ndim)]) for position in (source, target)]
    chosen = jax.random.permutation(stream_key, shards_of)[partner]
    strong = (owner == chosen) | (owner == (partner + shards_of // 2) % shards_of)
    return jnp.where(strong, factor * values, values)


def steps_of(own_key, shape, split, least, high):
    loudness = 1.0
    for position, blocks in split:
        draws = jax.random.uniform(jax.random.fold_in(jax.random.fold_in(own_key, 6), position), (blocks,), jnp.float32, least / len(split), high / len(split))
        loudness = loudness * jnp.repeat(jnp.exp(draws), shape[position] // blocks).reshape((-1,) + (1,) * (len(shape) - 1 - position))
    return loudness


def normal_values(own_key, dims, scale, reach, pieces=(), held_as=jnp.bfloat16):
    loudness = steps_of(own_key, dims, pieces, -0.22, 0.18) if pieces else 1.0
    result = jax.random.normal(own_key, dims, jnp.float32) * scale * loudness
    return jnp.minimum(jnp.maximum(result, -reach), reach).astype(held_as)


def bell_draw_with(key, dims, scale, bound, cuts, heavy, kind=jnp.bfloat16):
    values = scale * jax.random.normal(key, dims, jnp.float32)
    if cuts:
        values = values * steps_of(key, dims, cuts, -0.22, 0.18)
    return jnp.clip(raised(values, jax.random.fold_in(key, 3), *heavy), -bound, bound).astype(kind)


def setup_inputs(seed: int = 0) -> dict:
    seeds = jax.random.split(jax.random.key(seed), 5)
    query_grads = normal_values(seeds[0], (NQ, F), 1.0, 6.0, ((0, 16), (1, 16)))
    train_grads = bell_draw_with(seeds[1], (NT, F), F ** -0.5, 0.03125, ((0, 16), (1, 16)), (1, 0, 16, 2.0))
    eigenvalues = jnp.clip(jnp.exp(math.log(5.0) - 4.6051702 * jax.random.uniform(seeds[2], (F,), jnp.float32) ** steps_of(seeds[2], (F,), ((0, 16),), -0.2, 0.2)), 0.05, 5.0)
    offsets = draw_offsets(jax.random.fold_in(seeds[4], 71), 0)
    return dict(query_grads=query_grads, train_grads=train_grads, eigenvalues=eigenvalues, offsets=offsets)


def reference(query_grads, train_grads, eigenvalues, offsets):
    width = eigenvalues.shape[0]
    feature_ids = jnp.arange(width, dtype=jnp.int32)
    onehot = ((feature_ids[:, None] >= offsets[None, :-1]) & (feature_ids[:, None] < offsets[None, 1:])).astype(jnp.float32)
    layer_sum = jnp.dot(eigenvalues, onehot, precision=lax.Precision.HIGHEST)
    total = jnp.sum(layer_sum)
    counts = (offsets[1:] - offsets[:-1]).astype(jnp.float32)
    damping = 0.05 * (layer_sum / counts + total / F)
    damp_feat = jnp.dot(onehot, damping, precision=lax.Precision.HIGHEST)
    weight = 1.0 / (eigenvalues + damp_feat)
    preconditioned = (train_grads.astype(jnp.float32) * weight[None, :]).astype(jnp.bfloat16)
    return lax.dot_general(preconditioned, query_grads, (((1,), (1,)), ((), ())), preferred_element_type=jnp.float32)
```

```python
import functools

import jax
import jax.numpy as jnp
from jax import lax
from jax.experimental import pallas as pl
from jax.experimental.pallas import tpu as pltpu
from jax.sharding import PartitionSpec as P

MESH = pl.DeviceIdType.MESH
F = 65536
LAYERS = 32
ZS = 8
FEATS = 16
CHIPS = 16
WIDTH = 4096
ROWS = 128
QROWS = 512
CHUNK = 32
PAIR = 2 * CHUNK
PAIRS = 16
STEPS = PAIRS - 2
QPARTS = 8
QCHUNK = QROWS // QPARTS
GROUP = 4
BOTH = 12


def rows(start, size):
    return pl.ds(pl.multiple_of(start, size), size)


def kernel(
    offs, q_hbm, t_hbm, e_hbm, out,
    g, w, qb, pb, rb, wt, eb, ls,
    own_recv, t_send, r_send, r_recv, l_send, l_recv,
    home_recv, home_send, away_recv, away_send, fwd_send,
    e_copy, e_send, e_recv, ls_send, ls_recv, o_send, o_recv,
):
    qi, fi = lax.axis_index("query"), lax.axis_index("feat")
    xh, z = qi // ZS, qi % ZS
    xl, y, c = fi // 8, (fi // 2) % 4, fi % 2
    slot = (xh * 2 + xl) * 4 + y
    native = c == xh
    foreign = c != xh
    right = (xh * ZS + (z + 1) % ZS, fi)
    left = (xh * ZS + (z + ZS - 1) % ZS, fi)
    sibling = (qi, fi + 1 - 2 * c)
    partner = ((1 - xh) * ZS + z, fi + 1 - 2 * c)

    def remote(src, dst, send, recv, device):
        return pltpu.make_async_remote_copy(
            src_ref=src, dst_ref=dst, send_sem=send, recv_sem=recv, device_id=device, device_id_type=MESH
        )

    def arrived(ref, sem):
        pltpu.make_async_copy(ref, ref, sem).wait()

    def loop(low, high, body):
        def step(i, carry):
            body(i)
            return carry

        lax.fori_loop(low, high, step, 0)

    def own_rows(i):
        return rows(i * CHUNK, CHUNK)

    def q_rows(i):
        return rows(i * QCHUNK, QCHUNK)

    def local_t(i):
        return pltpu.make_async_copy(t_hbm.at[own_rows(i)], g.at[own_rows(i)], own_recv.at[i])

    def local_q(i):
        return pltpu.make_async_copy(q_hbm.at[q_rows(i)], qb.at[0, q_rows(i)], home_recv.at[i])

    local_e = pltpu.make_async_copy(e_hbm, eb.at[c], e_copy)
    local_e.start()

    @pl.when(native)
    def _():
        loop(0, 4, lambda i: local_t(i).start())

    barrier = pltpu.get_barrier_semaphore()
    for device in (left, right):
        pl.semaphore_signal(barrier, inc=1, device_id=device, device_id_type=MESH)

    def greet(i):
        device = (((xh + i // FEATS) % 2) * ZS + z, (fi + i) % FEATS)
        pl.semaphore_signal(barrier, inc=1, device_id=device, device_id_type=MESH)

    loop(1, 2 * FEATS, greet)
    pl.semaphore_wait(barrier, 2 * FEATS + 1)

    def swap_t(i):
        return remote(t_hbm.at[own_rows(i)], g.at[own_rows(i)], t_send.at[i], own_recv.at[i], partner)

    def swap_q(i):
        return remote(q_hbm.at[q_rows(i)], qb.at[1, q_rows(i)], away_send.at[i], away_recv.at[i], partner)

    def pass_q(i):
        return remote(qb.at[1, q_rows(i)], qb.at[1, q_rows(i)], fwd_send.at[i], away_recv.at[i], sibling)

    def share_q(i):
        return remote(q_hbm.at[q_rows(i)], qb.at[0, q_rows(i)], home_send.at[i], home_recv.at[i], sibling)

    def to_right(j, src):
        return remote(g.at[rows(src, CHUNK)], g.at[rows((j + 2) * PAIR, CHUNK)], r_send.at[j], r_recv.at[j], right)

    def to_left(j, src):
        return remote(g.at[rows(src, CHUNK)], g.at[rows((j + 2) * PAIR + CHUNK, CHUNK)], l_send.at[j], l_recv.at[j], left)

    def first_chunk(i):
        arrived(g.at[own_rows(i)], own_recv.at[i])
        to_right(i, i * CHUNK).start()
        to_left(i, i * CHUNK).start()

    @pl.when(foreign)
    def _():
        loop(0, 4, lambda i: swap_t(i).start())

    @pl.when(native)
    def _():
        loop(0, 4, first_chunk)

    share_e = remote(e_hbm, eb.at[c], e_send, e_recv, sibling)
    share_e.start()

    @pl.when(native)
    def _():
        def share(i):
            local_q(i).start()
            share_q(i).start()

        loop(0, QPARTS, share)

    layer = lax.broadcasted_iota(jnp.int32, (LAYERS, 128), 0)
    lane = lax.broadcasted_iota(jnp.int32, (LAYERS, 128), 1)
    low = jnp.zeros((LAYERS, 128), jnp.int32)
    high = jnp.zeros((LAYERS, 128), jnp.int32)
    for n in range(LAYERS):
        low = jnp.where(layer == n, offs[n], low)
        high = jnp.where(layer == n, offs[n + 1], high)

    def member(first):
        ids = lane + first
        return (ids >= low) & (ids < high)

    local_e.wait()

    def add_tile(i, acc):
        tile = eb[c, :, rows(i * 128, 128)]
        return acc + jnp.where(member(fi * WIDTH + i * 128), tile, 0.0)

    ls[fi] = lax.fori_loop(0, WIDTH // 128, add_tile, jnp.zeros((LAYERS, 128), jnp.float32))

    def share_sums(i):
        return remote(ls.at[fi], ls.at[fi], ls_send.at[i], ls_recv.at[fi], (qi, (fi + i) % FEATS))

    loop(1, FEATS, lambda i: share_sums(i).start())

    @pl.when(foreign)
    def _():
        first_chunk(0)
        first_chunk(1)
        swap_q(0).start()
        first_chunk(2)
        swap_q(1).start()
        first_chunk(3)
        swap_q(2).start()

    def take_sums(i):
        source = (fi + i) % FEATS
        arrived(ls.at[source], ls_recv.at[source])

    loop(1, FEATS, take_sums)
    layer_sum = jnp.sum(jnp.sum(ls[...], axis=0), axis=1, keepdims=True)
    total = jnp.sum(layer_sum, axis=0, keepdims=True)
    counts = (high - low).astype(jnp.float32)
    damping = 0.05 * (layer_sum / counts + total / F)

    arrived(eb.at[1 - c], e_recv)
    first_feature = (xl * 8 + y * 2 + xh) * WIDTH

    def weigh(i):
        at = rows(i * 128, 128)
        damp = jnp.sum(jnp.where(member(first_feature + i * 128), damping, 0.0), axis=0, keepdims=True)
        wt[:, at] = 1.0 / (eb[xh, :, at] + damp)

    loop(0, WIDTH // 128, weigh)

    def score_copies(p, side, half):
        distance = (p + 2) // 4
        source_z = (z + ZS + (2 * side - 1) * distance) % ZS
        part = jnp.where(p < 2, 2 * p + side, (p + 2) % 4 + 2 * side * (p // 14))
        device = (((xh + half) % 2) * ZS + z, c * 8 + source_z)
        src = pb.at[half, rows(p * PAIR + side * CHUNK, CHUNK)]
        dst = rb.at[slot, rows(part * CHUNK, CHUNK)]
        recv = o_recv.at[slot * 4 + part]
        send = o_send.at[half * (2 * PAIRS) + 2 * p + side]
        mine = jnp.logical_and(half == 0, fi == c * 8 + source_z)
        return mine, src, dst, send, recv, device

    def send_scores(p, side, half):
        mine, src, dst, send, recv, device = score_copies(p, side, half)

        @pl.when(mine)
        def _():
            pltpu.make_async_copy(src, dst, recv).start()

        @pl.when(jnp.logical_not(mine))
        def _():
            remote(src, dst, send, recv, device).start()

    def multiply(start, size, half):
        for n in range(QROWS // 256):
            scores = lax.dot_general(
                w[rows(start, size), :],
                qb[half, n * 256 : (n + 1) * 256, :],
                (((1,), (1,)), ((), ())),
                preferred_element_type=jnp.float32,
            )
            pb[half, rows(start, size), n * 256 : (n + 1) * 256] = scores.astype(jnp.bfloat16)

    def backlog(b):
        multiply(b * (GROUP * PAIR), GROUP * PAIR, 1)

        def send_both(i):
            send_scores(b * GROUP + i // 2, i % 2, 1)

        loop(0, 2 * GROUP, send_both)

    loop(0, QPARTS, lambda i: arrived(qb.at[0, q_rows(i)], home_recv.at[i]))

    def work(p):
        k = p - 2

        @pl.when(p >= 2)
        def _():
            arrived(g.at[rows(p * PAIR, CHUNK)], r_recv.at[k])
            arrived(g.at[rows(p * PAIR + CHUNK, CHUNK)], l_recv.at[k])

        @pl.when(jnp.logical_and(p >= 4, p < 14))
        def _():
            to_right(p, (p - 2) * PAIR).start()
            to_left(p, (p - 2 + 2 * (p // 12)) * PAIR + CHUNK).start()

        @pl.when(jnp.logical_and(foreign, jnp.logical_and(p >= 2, p < 7)))
        def _():
            swap_q(p - 2).wait_send()
            swap_q(p + 1).start()

        @pl.when(jnp.logical_and(foreign, jnp.logical_and(p >= 5, p < 13)))
        def _():
            arrived(qb.at[1, q_rows(p - 5)], away_recv.at[p - 5])
            pass_q(p - 5).start()

        def weight_rows(i):
            at = rows(i * 512, 512)
            raw = g[rows(p * PAIR, PAIR), at].astype(jnp.float32)
            w[rows(p * PAIR, PAIR), at] = (raw * wt[:, at]).astype(jnp.bfloat16)

        loop(0, WIDTH // 512, weight_rows)

        @pl.when(jnp.logical_and(native, p == BOTH))
        def _():
            loop(0, QPARTS, lambda i: arrived(qb.at[1, q_rows(i)], away_recv.at[i]))

        def one_half(half):
            multiply(p * PAIR, PAIR, half)
            send_scores(p, 0, half)
            send_scores(p, 1, half)

        loop(0, 1 + p // BOTH, one_half)

        @pl.when(p == BOTH)
        def _():
            loop(0, 2, backlog)

        @pl.when(p == BOTH + 1)
        def _():
            backlog(2)

    loop(0, PAIRS, work)

    def drain_scores(i):
        mine, src, dst, send, recv, device = score_copies((i % 32) // 2, i % 2, i // 32)

        @pl.when(jnp.logical_not(mine))
        def _():
            remote(src, dst, send, recv, device).wait_send()

    def drain_ring(j):
        to_right(j, 0).wait_send()
        to_left(j, 0).wait_send()

    loop(0, STEPS, drain_ring)
    loop(1, FEATS, lambda i: share_sums(i).wait_send())
    share_e.wait_send()

    @pl.when(native)
    def _():
        loop(0, QPARTS, lambda i: share_q(i).wait_send())

    @pl.when(foreign)
    def _():
        loop(0, 4, lambda i: swap_t(i).wait_send())
        loop(5, QPARTS, lambda i: swap_q(i).wait_send())
        loop(0, QPARTS, lambda i: pass_q(i).wait_send())

    loop(0, 4 * PAIRS, drain_scores)

    def finish(i):
        part = (i % 2) * 2 + i // 2
        at = rows(part * CHUNK, CHUNK)
        out[at, :] = jnp.zeros((CHUNK, QROWS), jnp.float32)

        def add(s):
            arrived(rb.at[s, at], o_recv.at[s * 4 + part])
            out[at, :] += rb[s, at, :].astype(jnp.float32)

        loop(0, CHIPS, add)

    loop(0, 4, finish)


def per_device(query_grads, train_grads, eigenvalues, offsets):
    dma = pltpu.SemaphoreType.DMA
    anywhere = pl.BlockSpec(memory_space=pl.ANY)
    return pl.pallas_call(
        kernel,
        out_shape=jax.ShapeDtypeStruct((ROWS, QROWS), jnp.float32),
        in_specs=[pl.BlockSpec(memory_space=pltpu.SMEM), anywhere, anywhere, anywhere],
        out_specs=pl.BlockSpec(memory_space=pltpu.VMEM),
        scratch_shapes=[
            pltpu.VMEM((PAIRS * PAIR, WIDTH), jnp.bfloat16),
            pltpu.VMEM((PAIRS * PAIR, WIDTH), jnp.bfloat16),
            pltpu.VMEM((2, QROWS, WIDTH), jnp.bfloat16),
            pltpu.VMEM((2, PAIRS * PAIR, QROWS), jnp.bfloat16),
            pltpu.VMEM((CHIPS, ROWS, QROWS), jnp.bfloat16),
            pltpu.VMEM((1, WIDTH), jnp.float32),
            pltpu.VMEM((2, 1, WIDTH), jnp.float32),
            pltpu.VMEM((FEATS, LAYERS, 128), jnp.float32),
            dma((4,)), dma((4,)),
            dma((STEPS,)), dma((STEPS,)), dma((STEPS,)), dma((STEPS,)),
            dma((QPARTS,)), dma((QPARTS,)), dma((QPARTS,)), dma((QPARTS,)), dma((QPARTS,)),
            dma, dma, dma,
            dma((FEATS,)), dma((FEATS,)),
            dma((4 * PAIRS,)), dma((4 * CHIPS,)),
        ],
        compiler_params=pltpu.CompilerParams(
            collective_id=0, has_side_effects=True, vmem_limit_bytes=56 * 2**20
        ),
        name="scores",
    )(offsets, query_grads, train_grads, eigenvalues.reshape(1, WIDTH))


def solution(mesh):
    return jax.shard_map(
        per_device,
        mesh=mesh,
        in_specs=(P("query", "feat"), P("query", "feat"), P("feat"), P()),
        out_specs=P("feat", "query"),
        check_vma=False,
    )
```

```python
import functools

import jax
import jax.numpy as jnp
from jax import lax
from jax.experimental import pallas as pl
from jax.experimental.pallas import tpu as pltpu
from jax.sharding import PartitionSpec as P

MESH = pl.DeviceIdType.MESH
F = 65536
LAYERS = 32
ZS = 8
FEATS = 16
CHIPS = 16
WIDTH = 4096
ROWS = 128
QROWS = 512
CHUNK = 32
PAIR = 2 * CHUNK
PAIRS = 16
STEPS = PAIRS - 2
QPARTS = 8
QCHUNK = QROWS // QPARTS
GROUP = 4
BOTH = 12


def rows(start, size):
    return pl.ds(pl.multiple_of(start, size), size)


def kernel(
    offs, q_hbm, t_hbm, e_hbm, out,
    g, w, qb, pb, rb, wt, eb, ls,
    own_recv, t_send, r_send, r_recv, l_send, l_recv,
    home_recv, home_send, away_recv, away_send, fwd_send,
    e_copy, e_send, e_recv, ls_send, ls_recv, o_send, o_recv,
):
    qi, fi = lax.axis_index("query"), lax.axis_index("feat")
    xh, z = qi // ZS, qi % ZS
    xl, y, c = fi // 8, (fi // 2) % 4, fi % 2
    slot = (xh * 2 + xl) * 4 + y
    native = c == xh
    foreign = c != xh
    right = (xh * ZS + (z + 1) % ZS, fi)
    left = (xh * ZS + (z + ZS - 1) % ZS, fi)
    sibling = (qi, fi + 1 - 2 * c)
    partner = ((1 - xh) * ZS + z, fi + 1 - 2 * c)

    def remote(src, dst, send, recv, device):
        return pltpu.make_async_remote_copy(
            src_ref=src, dst_ref=dst, send_sem=send, recv_sem=recv, device_id=device, device_id_type=MESH
        )

    def arrived(ref, sem):
        pltpu.make_async_copy(ref, ref, sem).wait()

    def loop(low, high, body):
        def step(i, carry):
            body(i)
            return carry

        lax.fori_loop(low, high, step, 0)

    def own_rows(i):
        return rows(i * CHUNK, CHUNK)

    def q_rows(i):
        return rows(i * QCHUNK, QCHUNK)

    def local_t(i):
        return pltpu.make_async_copy(t_hbm.at[own_rows(i)], g.at[own_rows(i)], own_recv.at[i])

    def local_q(i):
        return pltpu.make_async_copy(q_hbm.at[q_rows(i)], qb.at[0, q_rows(i)], home_recv.at[i])

    local_e = pltpu.make_async_copy(e_hbm, eb.at[c], e_copy)
    local_e.start()

    @pl.when(native)
    def _():
        loop(0, 4, lambda i: local_t(i).start())

    barrier = pltpu.get_barrier_semaphore()
    for device in (left, right):
        pl.semaphore_signal(barrier, inc=1, device_id=device, device_id_type=MESH)

    def greet(i):
        device = (((xh + i // FEATS) % 2) * ZS + z, (fi + i) % FEATS)
        pl.semaphore_signal(barrier, inc=1, device_id=device, device_id_type=MESH)

    loop(1, 2 * FEATS, greet)
    pl.semaphore_wait(barrier, 2 * FEATS + 1)

    def swap_t(i):
        return remote(t_hbm.at[own_rows(i)], g.at[own_rows(i)], t_send.at[i], own_recv.at[i], partner)

    def swap_q(i):
        return remote(q_hbm.at[q_rows(i)], qb.at[1, q_rows(i)], away_send.at[i], away_recv.at[i], partner)

    def pass_q(i):
        return remote(qb.at[1, q_rows(i)], qb.at[1, q_rows(i)], fwd_send.at[i], away_recv.at[i], sibling)

    def share_q(i):
        return remote(q_hbm.at[q_rows(i)], qb.at[0, q_rows(i)], home_send.at[i], home_recv.at[i], sibling)

    def to_right(j, src):
        return remote(g.at[rows(src, CHUNK)], g.at[rows((j + 2) * PAIR, CHUNK)], r_send, r_recv.at[j], right)

    def to_left(j, src):
        return remote(g.at[rows(src, CHUNK)], g.at[rows((j + 2) * PAIR + CHUNK, CHUNK)], l_send, l_recv.at[j], left)

    def first_chunk(i):
        arrived(g.at[own_rows(i)], own_recv.at[i])
        to_right(i, i * CHUNK).start()
        to_left((i + 2) % 4, i * CHUNK).start()

    @pl.when(foreign)
    def _():
        for i in (0, 2, 1, 3):
            swap_t(i).start()

    @pl.when(native)
    def _():
        for i in (0, 2, 1, 3):
            first_chunk(i)

    share_e = remote(e_hbm, eb.at[c], e_send, e_recv, sibling)
    share_e.start()

    @pl.when(native)
    def _():
        def share(i):
            local_q(i).start()
            share_q(i).start()

        loop(0, QPARTS, share)

    layer = lax.broadcasted_iota(jnp.int32, (LAYERS, 128), 0)
    lane = lax.broadcasted_iota(jnp.int32, (LAYERS, 128), 1)
    low = jnp.zeros((LAYERS, 128), jnp.int32)
    high = jnp.zeros((LAYERS, 128), jnp.int32)
    for n in range(LAYERS):
        low = jnp.where(layer == n, offs[n], low)
        high = jnp.where(layer == n, offs[n + 1], high)

    def member(first):
        ids = lane + first
        return (ids >= low) & (ids < high)

    local_e.wait()

    def add_tile(i, acc):
        tile = eb[c, :, rows(i * 128, 128)]
        return acc + jnp.where(member(fi * WIDTH + i * 128), tile, 0.0)

    ls[fi] = lax.fori_loop(0, WIDTH // 128, add_tile, jnp.zeros((LAYERS, 128), jnp.float32))

    def share_sums(i):
        return remote(ls.at[fi], ls.at[fi], ls_send, ls_recv, (qi, (fi + i) % FEATS))

    loop(1, FEATS, lambda i: share_sums(i).start())

    @pl.when(foreign)
    def _():
        first_chunk(0)
        first_chunk(2)
        swap_q(0).start()
        first_chunk(1)
        swap_q(1).start()
        first_chunk(3)
        swap_q(2).start()

    arrived(ls.at[pl.ds(0, FEATS - 1)], ls_recv)
    layer_sum = jnp.sum(jnp.sum(ls[...], axis=0), axis=1, keepdims=True)
    total = jnp.sum(layer_sum, axis=0, keepdims=True)
    counts = (high - low).astype(jnp.float32)
    damping = 0.05 * (layer_sum / counts + total / F)

    arrived(eb.at[1 - c], e_recv)
    first_feature = (xl * 8 + y * 2 + xh) * WIDTH

    def weigh(i):
        at = rows(i * 128, 128)
        damp = jnp.sum(jnp.where(member(first_feature + i * 128), damping, 0.0), axis=0, keepdims=True)
        wt[:, at] = 1.0 / (eb[xh, :, at] + damp)

    loop(0, WIDTH // 128, weigh)

    def score_copies(p, side, half):
        late = p // 12
        distance = jnp.where(late > 0, 4 - p % 2, (p + 2) // 4)
        number = jnp.where(late > 0, p % 2 * 2 + (p - 12) // 2, (p + 2) % 4)
        source_z = (z + ZS + (2 * side - 1) * distance) % ZS
        part = jnp.where(p < 2, 2 * p + side, (number + 2 * side) % 4)
        device = (((xh + half) % 2) * ZS + z, c * 8 + source_z)
        src = pb.at[half, rows(p * PAIR + side * CHUNK, CHUNK)]
        dst = rb.at[slot, rows(part * CHUNK, CHUNK)]
        recv = o_recv.at[part]
        send = o_send
        mine = jnp.logical_and(half == 0, fi == c * 8 + source_z)
        return mine, src, dst, send, recv, device

    def send_scores(p, side, half):
        mine, src, dst, send, recv, device = score_copies(p, side, half)

        @pl.when(mine)
        def _():
            pltpu.make_async_copy(src, dst, recv).start()

        @pl.when(jnp.logical_not(mine))
        def _():
            remote(src, dst, send, recv, device).start()

    def multiply(start, size, half):
        at = pl.ds(pl.multiple_of(start, PAIR), size)
        for n in range(QROWS // 256):
            scores = lax.dot_general(
                w[at, :],
                qb[half, n * 256 : (n + 1) * 256, :],
                (((1,), (1,)), ((), ())),
                preferred_element_type=jnp.float32,
            )
            pb[half, at, n * 256 : (n + 1) * 256] = scores.astype(jnp.bfloat16)

    def backlog(b, size=GROUP):
        multiply(b * (GROUP * PAIR), size * PAIR, 1)

        def send_both(i):
            send_scores(b * GROUP + i // 2, i % 2, 1)

        loop(0, 2 * size, send_both)

    loop(0, QPARTS, lambda i: arrived(qb.at[0, q_rows(i)], home_recv.at[i]))

    def work(p):
        k = p - 2

        @pl.when(p >= 2)
        def _():
            arrived(g.at[rows(p * PAIR, CHUNK)], r_recv.at[k])
            arrived(g.at[rows(p * PAIR + CHUNK, CHUNK)], l_recv.at[k])

        def pass_on(j, pair):
            to_right(j, pair * PAIR).start()
            to_left(j, pair * PAIR + CHUNK).start()

        @pl.when(jnp.logical_and(p >= 2, p < 8))
        def _():
            pass_on(p + 2, p)

        @pl.when(jnp.logical_or(p == 10, p == 11))
        def _():
            pass_on(2 * p - 10, p)
            pass_on(2 * p - 9, p - 2)

        @pl.when(jnp.logical_and(foreign, jnp.logical_and(p >= 2, p < 7)))
        def _():
            swap_q(p - 2).wait_send()
            swap_q(p + 1).start()

        @pl.when(jnp.logical_and(foreign, jnp.logical_and(p >= 5, p < 13)))
        def _():
            arrived(qb.at[1, q_rows(p - 5)], away_recv.at[p - 5])
            pass_q(p - 5).start()

        def weight_rows(i):
            at = rows(i * 512, 512)
            raw = g[rows(p * PAIR, PAIR), at].astype(jnp.float32)
            w[rows(p * PAIR, PAIR), at] = (raw * wt[:, at]).astype(jnp.bfloat16)

        loop(0, WIDTH // 512, weight_rows)

        @pl.when(jnp.logical_and(native, p == BOTH))
        def _():
            loop(0, QPARTS, lambda i: arrived(qb.at[1, q_rows(i)], away_recv.at[i]))

        def one_half(half):
            multiply(p * PAIR, PAIR, half)
            send_scores(p, 0, half)
            send_scores(p, 1, half)

        loop(0, 1 + p // BOTH, one_half)

        @pl.when(p == BOTH)
        def _():
            loop(0, 2, backlog)

        @pl.when(p == BOTH + 1)
        def _():
            backlog(2, BOTH - 2 * GROUP)

    loop(0, PAIRS, work)

    for part in (0, 2, 1, 3):
        at = pl.ds(part * CHUNK, CHUNK)
        arrived(rb.at[:, at], o_recv.at[part])
        total = rb[0, at, :].astype(jnp.float32)
        for source in range(1, CHIPS):
            total += rb[source, at, :].astype(jnp.float32)
        out[at, :] = total

    sent = pl.ds(0, STEPS * CHUNK)
    arrived(g.at[sent], r_send)
    arrived(g.at[sent], l_send)
    arrived(pb.at[0], o_send)
    arrived(pb.at[1, pl.ds(0, (PAIRS - 2) * PAIR)], o_send)

    @pl.when(xl != c)
    def _():
        arrived(pb.at[1, pl.ds((PAIRS - 2) * PAIR, 2 * PAIR)], o_send)

    arrived(ls.at[pl.ds(0, FEATS - 1)], ls_send)
    share_e.wait_send()

    @pl.when(native)
    def _():
        loop(0, QPARTS, lambda i: share_q(i).wait_send())

    @pl.when(foreign)
    def _():
        loop(0, 4, lambda i: swap_t(i).wait_send())
        loop(5, QPARTS, lambda i: swap_q(i).wait_send())
        loop(0, QPARTS, lambda i: pass_q(i).wait_send())


def per_device(query_grads, train_grads, eigenvalues, offsets):
    dma = pltpu.SemaphoreType.DMA
    anywhere = pl.BlockSpec(memory_space=pl.ANY)
    return pl.pallas_call(
        kernel,
        out_shape=jax.ShapeDtypeStruct((ROWS, QROWS), jnp.float32),
        in_specs=[pl.BlockSpec(memory_space=pltpu.SMEM), anywhere, anywhere, anywhere],
        out_specs=pl.BlockSpec(memory_space=pltpu.VMEM),
        scratch_shapes=[
            pltpu.VMEM((PAIRS * PAIR, WIDTH), jnp.bfloat16),
            pltpu.VMEM((PAIRS * PAIR, WIDTH), jnp.bfloat16),
            pltpu.VMEM((2, QROWS, WIDTH), jnp.bfloat16),
            pltpu.VMEM((2, PAIRS * PAIR, QROWS), jnp.bfloat16),
            pltpu.VMEM((CHIPS, ROWS, QROWS), jnp.bfloat16),
            pltpu.VMEM((1, WIDTH), jnp.float32),
            pltpu.VMEM((2, 1, WIDTH), jnp.float32),
            pltpu.VMEM((FEATS, LAYERS, 128), jnp.float32),
            dma((4,)), dma((4,)),
            dma, dma((STEPS,)), dma, dma((STEPS,)),
            dma((QPARTS,)), dma((QPARTS,)), dma((QPARTS,)), dma((QPARTS,)), dma((QPARTS,)),
            dma, dma, dma,
            dma, dma,
            dma, dma((4,)),
        ],
        compiler_params=pltpu.CompilerParams(
            collective_id=0, has_side_effects=True, vmem_limit_bytes=56 * 2**20
        ),
        name="scores",
    )(offsets, query_grads, train_grads, eigenvalues.reshape(1, WIDTH))


def solution(mesh):
    return jax.shard_map(
        per_device,
        mesh=mesh,
        in_specs=(P("query", "feat"), P("query", "feat"), P("feat"), P()),
        out_specs=P("feat", "query"),
        check_vma=False,
    )
```

```python
import functools

import jax
import jax.numpy as jnp
from jax import lax
from jax.experimental import pallas as pl
from jax.experimental.pallas import tpu as pltpu
from jax.sharding import PartitionSpec as P

MESH = pl.DeviceIdType.MESH
F = 65536
LAYERS = 32
ZS = 8
FEATS = 16
CHIPS = 16
WIDTH = 4096
ROWS = 128
QROWS = 512
CHUNK = 32
PAIR = 2 * CHUNK
PAIRS = 16
STEPS = PAIRS - 2
QPARTS = 8
QCHUNK = QROWS // QPARTS
GROUP = 4
SOME = 8
BOTH = 12


def rows(start, size):
    return pl.ds(pl.multiple_of(start, size), size)


def kernel(
    offs, q_hbm, t_hbm, e_hbm, out,
    g, w, qb, pb, rb, wt, eb, ls,
    own_recv, t_send, r_send, r_recv, l_send, l_recv,
    home_recv, home_send, away_recv, away_send, fwd_send,
    e_copy, e_send, e_recv, ls_send, ls_recv, o_send, o_recv,
):
    qi, fi = lax.axis_index("query"), lax.axis_index("feat")
    xh, z = qi // ZS, qi % ZS
    xl, y, c = fi // 8, (fi // 2) % 4, fi % 2
    slot = (xh * 2 + xl) * 4 + y
    native = c == xh
    foreign = c != xh
    right = (xh * ZS + (z + 1) % ZS, fi)
    left = (xh * ZS + (z + ZS - 1) % ZS, fi)
    sibling = (qi, fi + 1 - 2 * c)
    partner = ((1 - xh) * ZS + z, fi + 1 - 2 * c)

    def remote(src, dst, send, recv, device):
        return pltpu.make_async_remote_copy(
            src_ref=src, dst_ref=dst, send_sem=send, recv_sem=recv, device_id=device, device_id_type=MESH
        )

    def arrived(ref, sem):
        pltpu.make_async_copy(ref, ref, sem).wait()

    def loop(low, high, body):
        def step(i, carry):
            body(i)
            return carry

        lax.fori_loop(low, high, step, 0)

    def own_rows(i):
        return rows(i * CHUNK, CHUNK)

    def q_rows(i):
        return rows(i * QCHUNK, QCHUNK)

    def local_t(i):
        return pltpu.make_async_copy(t_hbm.at[own_rows(i)], g.at[own_rows(i)], own_recv.at[i])

    def local_q(i):
        return pltpu.make_async_copy(q_hbm.at[q_rows(i)], qb.at[0, q_rows(i)], home_recv.at[i])

    local_e = pltpu.make_async_copy(e_hbm, eb.at[c], e_copy)
    local_e.start()

    @pl.when(native)
    def _():
        loop(0, 4, lambda i: local_t(i).start())

    barrier = pltpu.get_barrier_semaphore()
    for device in (left, right):
        pl.semaphore_signal(barrier, inc=1, device_id=device, device_id_type=MESH)

    def greet(i):
        device = (((xh + i // FEATS) % 2) * ZS + z, (fi + i) % FEATS)
        pl.semaphore_signal(barrier, inc=1, device_id=device, device_id_type=MESH)

    loop(1, 2 * FEATS, greet)
    pl.semaphore_wait(barrier, 2 * FEATS + 1)

    def swap_t(i):
        return remote(t_hbm.at[own_rows(i)], g.at[own_rows(i)], t_send.at[i], own_recv.at[i], partner)

    def swap_q(i):
        return remote(q_hbm.at[q_rows(i)], qb.at[1, q_rows(i)], away_send.at[i], away_recv.at[i], partner)

    def pass_q(i):
        return remote(qb.at[1, q_rows(i)], qb.at[1, q_rows(i)], fwd_send.at[i], away_recv.at[i], sibling)

    def share_q(i):
        return remote(q_hbm.at[q_rows(i)], qb.at[0, q_rows(i)], home_send.at[i], home_recv.at[i], sibling)

    def to_right(j, src):
        return remote(g.at[rows(src, CHUNK)], g.at[rows((j + 2) * PAIR, CHUNK)], r_send, r_recv.at[j], right)

    def to_left(j, src):
        return remote(g.at[rows(src, CHUNK)], g.at[rows((j + 2) * PAIR + CHUNK, CHUNK)], l_send, l_recv.at[j], left)

    def first_chunk(i):
        arrived(g.at[own_rows(i)], own_recv.at[i])
        to_right(i, i * CHUNK).start()
        to_left((i + 2) % 4, i * CHUNK).start()

    @pl.when(foreign)
    def _():
        for i in (0, 2, 1, 3):
            swap_t(i).start()

    @pl.when(native)
    def _():
        for i in (0, 2, 1, 3):
            first_chunk(i)

    share_e = remote(e_hbm, eb.at[c], e_send, e_recv, sibling)
    share_e.start()

    @pl.when(native)
    def _():
        def share(i):
            local_q(i).start()
            share_q(i).start()

        loop(0, QPARTS, share)

    layer = lax.broadcasted_iota(jnp.int32, (LAYERS, 128), 0)
    lane = lax.broadcasted_iota(jnp.int32, (LAYERS, 128), 1)
    low = jnp.zeros((LAYERS, 128), jnp.int32)
    high = jnp.zeros((LAYERS, 128), jnp.int32)
    for n in range(LAYERS):
        low = jnp.where(layer == n, offs[n], low)
        high = jnp.where(layer == n, offs[n + 1], high)

    def member(first):
        ids = lane + first
        return (ids >= low) & (ids < high)

    local_e.wait()

    def add_tile(i, acc):
        tile = eb[c, :, rows(i * 128, 128)]
        return acc + jnp.where(member(fi * WIDTH + i * 128), tile, 0.0)

    ls[fi] = lax.fori_loop(0, WIDTH // 128, add_tile, jnp.zeros((LAYERS, 128), jnp.float32))

    def share_sums(i):
        return remote(ls.at[fi], ls.at[fi], ls_send, ls_recv, (qi, (fi + i) % FEATS))

    loop(1, FEATS, lambda i: share_sums(i).start())

    @pl.when(foreign)
    def _():
        first_chunk(0)
        first_chunk(2)
        swap_q(0).start()
        first_chunk(1)
        swap_q(1).start()
        first_chunk(3)
        swap_q(2).start()

    arrived(ls.at[pl.ds(0, FEATS - 1)], ls_recv)
    layer_sum = jnp.sum(jnp.sum(ls[...], axis=0), axis=1, keepdims=True)
    total = jnp.sum(layer_sum, axis=0, keepdims=True)
    counts = (high - low).astype(jnp.float32)
    damping = 0.05 * (layer_sum / counts + total / F)

    arrived(eb.at[1 - c], e_recv)
    first_feature = (xl * 8 + y * 2 + xh) * WIDTH

    def weigh(i):
        at = rows(i * 128, 128)
        damp = jnp.sum(jnp.where(member(first_feature + i * 128), damping, 0.0), axis=0, keepdims=True)
        wt[:, at] = 1.0 / (eb[xh, :, at] + damp)

    loop(0, WIDTH // 128, weigh)

    def send_scores(p, side, half, columns=pl.ds(0, QROWS)):
        late = p // 12
        distance = jnp.where(late > 0, 4 - p % 2, (p + 2) // 4)
        number = jnp.where(late > 0, p % 2 * 2 + (p - 12) // 2, (p + 2) % 4)
        source_z = (z + ZS + (2 * side - 1) * distance) % ZS
        part = jnp.where(p < 2, 2 * p + side, (number + 2 * side) % 4)
        mine = jnp.logical_and(half == 0, fi == c * 8 + source_z)
        src = pb.at[half, rows(p * PAIR + side * CHUNK, CHUNK), columns]
        dst = rb.at[slot, rows(part * CHUNK, CHUNK), columns]

        @pl.when(mine)
        def _():
            pltpu.make_async_copy(src, dst, o_recv.at[part]).start()

        @pl.when(jnp.logical_not(mine))
        def _():
            device = (((xh + half) % 2) * ZS + z, c * 8 + source_z)
            remote(src, dst, o_send, o_recv.at[part], device).start()

    def multiply(start, size, block):
        half, at, columns = block // 2, pl.ds(pl.multiple_of(start, PAIR), size), rows(block % 2 * 256, 256)
        scores = lax.dot_general(
            w[at, :], qb[half, columns, :], (((1,), (1,)), ((), ())), preferred_element_type=jnp.float32
        )
        pb[half, at, columns] = scores.astype(jnp.bfloat16)

    near = 1 - z % 2

    def order(n, turn):
        ring = jnp.where(n < 8, n - 2, jnp.where(n < turn, n - 6, jnp.where(n < 22, n - turn + 6, n - 12)))
        same = jnp.logical_or(n < 8, jnp.logical_and(n >= turn, n < 22))
        return jnp.where(n < 4, n // 2, ring), jnp.where(n < 4, n % 2, jnp.where(same, near, 1 - near))

    def backlog(groups, block):
        loop(0, groups, lambda b: multiply(b * (GROUP * PAIR), GROUP * PAIR, block))
        count = 2 * GROUP * groups

        def send(i):
            p, side = order((i + count // 4 * y) % count, 14 if groups == 2 else 16)
            send_scores(p, side, 1, pl.ds(block % 2 * 256, 256))

        loop(0, count, send)

    loop(0, QPARTS, lambda i: arrived(qb.at[0, q_rows(i)], home_recv.at[i]))

    def work(p):
        k = p - 2

        @pl.when(p >= 2)
        def _():
            arrived(g.at[rows(p * PAIR, CHUNK)], r_recv.at[k])
            arrived(g.at[rows(p * PAIR + CHUNK, CHUNK)], l_recv.at[k])

        def pass_on(j, pair):
            to_right(j, pair * PAIR).start()
            to_left(j, pair * PAIR + CHUNK).start()

        @pl.when(jnp.logical_and(p >= 2, p < 8))
        def _():
            pass_on(p + 2, p)

        @pl.when(jnp.logical_or(p == 10, p == 11))
        def _():
            pass_on(2 * p - 10, p)
            pass_on(2 * p - 9, p - 2)

        @pl.when(jnp.logical_and(foreign, jnp.logical_and(p >= 2, p < 7)))
        def _():
            swap_q(p - 2).wait_send()
            swap_q(p + 1).start()

        @pl.when(jnp.logical_and(foreign, jnp.logical_and(p >= 4, p < 12)))
        def _():
            arrived(qb.at[1, q_rows(p - 4)], away_recv.at[p - 4])
            pass_q(p - 4).start()

        def weight_rows(i):
            at = rows(i * 512, 512)
            raw = g[rows(p * PAIR, PAIR), at].astype(jnp.float32)
            w[rows(p * PAIR, PAIR), at] = (raw * wt[:, at]).astype(jnp.bfloat16)

        loop(0, WIDTH // 512, weight_rows)

        @pl.when(jnp.logical_and(native, p == SOME))
        def _():
            loop(0, QPARTS // 2, lambda i: arrived(qb.at[1, q_rows(i)], away_recv.at[i]))

        @pl.when(jnp.logical_and(native, p == BOTH))
        def _():
            loop(QPARTS // 2, QPARTS, lambda i: arrived(qb.at[1, q_rows(i)], away_recv.at[i]))

        def one_block(block):
            multiply(p * PAIR, PAIR, block)

            @pl.when(block % 2 == 1)
            def _():
                send_scores(p, 0, block // 2)
                send_scores(p, 1, block // 2)

            @pl.when(jnp.logical_and(block == 2, p < BOTH))
            def _():
                send_scores(p, 0, 1, pl.ds(0, 256))
                send_scores(p, 1, 1, pl.ds(0, 256))

        loop(0, 2 + p // SOME + p // BOTH, one_block)

        @pl.when(p == SOME)
        def _():
            backlog(SOME // GROUP, 2)

        @pl.when(p == BOTH)
        def _():
            backlog(BOTH // GROUP, 3)

    loop(0, PAIRS, work)

    for part in (0, 2, 1, 3):
        at = pl.ds(part * CHUNK, CHUNK)
        arrived(rb.at[:, at], o_recv.at[part])
        total = rb[0, at, :].astype(jnp.float32)
        for source in range(1, CHIPS):
            total += rb[source, at, :].astype(jnp.float32)
        out[at, :] = total

    sent = pl.ds(0, STEPS * CHUNK)
    arrived(g.at[sent], r_send)
    arrived(g.at[sent], l_send)
    arrived(pb.at[0], o_send)
    arrived(pb.at[1, pl.ds(0, (PAIRS - 2) * PAIR)], o_send)

    @pl.when(xl != c)
    def _():
        arrived(pb.at[1, pl.ds((PAIRS - 2) * PAIR, 2 * PAIR)], o_send)

    arrived(ls.at[pl.ds(0, FEATS - 1)], ls_send)
    share_e.wait_send()

    @pl.when(native)
    def _():
        loop(0, QPARTS, lambda i: share_q(i).wait_send())

    @pl.when(foreign)
    def _():
        loop(0, 4, lambda i: swap_t(i).wait_send())
        loop(5, QPARTS, lambda i: swap_q(i).wait_send())
        loop(0, QPARTS, lambda i: pass_q(i).wait_send())


def per_device(query_grads, train_grads, eigenvalues, offsets):
    dma = pltpu.SemaphoreType.DMA
    anywhere = pl.BlockSpec(memory_space=pl.ANY)
    return pl.pallas_call(
        kernel,
        out_shape=jax.ShapeDtypeStruct((ROWS, QROWS), jnp.float32),
        in_specs=[pl.BlockSpec(memory_space=pltpu.SMEM), anywhere, anywhere, anywhere],
        out_specs=pl.BlockSpec(memory_space=pltpu.VMEM),
        scratch_shapes=[
            pltpu.VMEM((PAIRS * PAIR, WIDTH), jnp.bfloat16),
            pltpu.VMEM((PAIRS * PAIR, WIDTH), jnp.bfloat16),
            pltpu.VMEM((2, QROWS, WIDTH), jnp.bfloat16),
            pltpu.VMEM((2, PAIRS * PAIR, QROWS), jnp.bfloat16),
            pltpu.VMEM((CHIPS, ROWS, QROWS), jnp.bfloat16),
            pltpu.VMEM((1, WIDTH), jnp.float32),
            pltpu.VMEM((2, 1, WIDTH), jnp.float32),
            pltpu.VMEM((FEATS, LAYERS, 128), jnp.float32),
            dma((4,)), dma((4,)),
            dma, dma((STEPS,)), dma, dma((STEPS,)),
            dma((QPARTS,)), dma((QPARTS,)), dma((QPARTS,)), dma((QPARTS,)), dma((QPARTS,)),
            dma, dma, dma,
            dma, dma,
            dma, dma((4,)),
        ],
        compiler_params=pltpu.CompilerParams(
            collective_id=0, has_side_effects=True, vmem_limit_bytes=56 * 2**20
        ),
        name="scores",
    )(offsets, query_grads, train_grads, eigenvalues.reshape(1, WIDTH))


def solution(mesh):
    return jax.shard_map(
        per_device,
        mesh=mesh,
        in_specs=(P("query", "feat"), P("query", "feat"), P("feat"), P()),
        out_specs=P("feat", "query"),
        check_vma=False,
    )
```

```python
import functools

import jax
import jax.numpy as jnp
from jax import lax
from jax.experimental import pallas as pl
from jax.experimental.pallas import tpu as pltpu
from jax.sharding import PartitionSpec as P

MESH = pl.DeviceIdType.MESH
F = 65536
LAYERS = 32
ZS = 8
FEATS = 16
CHIPS = 16
WIDTH = 4096
ROWS = 128
QROWS = 512
CHUNK = 32
PAIR = 2 * CHUNK
PAIRS = 16
STEPS = PAIRS - 2
QPARTS = 8
QCHUNK = QROWS // QPARTS
GROUP = 4
SOME = 8
BOTH = 12


def rows(start, size):
    return pl.ds(pl.multiple_of(start, size), size)


def kernel(
    offs, q_hbm, t_hbm, e_hbm, out,
    g, w, qb, pb, rb, wt, eb, ls,
    own_recv, t_send, r_send, r_recv, l_send, l_recv,
    home_recv, home_send, away_recv, away_send, fwd_send,
    e_copy, e_send, e_recv, ls_send, ls_recv, o_send, o_recv,
):
    qi, fi = lax.axis_index("query"), lax.axis_index("feat")
    xh, z = qi // ZS, qi % ZS
    xl, y, c = fi // 8, (fi // 2) % 4, fi % 2
    slot = (xh * 2 + xl) * 4 + y
    native = c == xh
    foreign = c != xh
    right = (xh * ZS + (z + 1) % ZS, fi)
    left = (xh * ZS + (z + ZS - 1) % ZS, fi)
    sibling = (qi, fi + 1 - 2 * c)
    partner = ((1 - xh) * ZS + z, fi + 1 - 2 * c)

    def remote(src, dst, send, recv, device):
        return pltpu.make_async_remote_copy(
            src_ref=src, dst_ref=dst, send_sem=send, recv_sem=recv, device_id=device, device_id_type=MESH
        )

    def arrived(ref, sem):
        pltpu.make_async_copy(ref, ref, sem).wait()

    def loop(low, high, body):
        def step(i, carry):
            body(i)
            return carry

        lax.fori_loop(low, high, step, 0)

    def own_rows(i):
        return rows(i * CHUNK, CHUNK)

    def q_rows(i):
        return rows(i * QCHUNK, QCHUNK)

    def local_t(i):
        return pltpu.make_async_copy(t_hbm.at[own_rows(i)], g.at[own_rows(i)], own_recv.at[i])

    def local_q(i):
        return pltpu.make_async_copy(q_hbm.at[q_rows(i)], qb.at[0, q_rows(i)], home_recv.at[i])

    local_e = pltpu.make_async_copy(e_hbm, eb.at[c], e_copy)
    local_e.start()

    @pl.when(native)
    def _():
        loop(0, 4, lambda i: local_t(i).start())

    barrier = pltpu.get_barrier_semaphore()
    for device in (left, right):
        pl.semaphore_signal(barrier, inc=1, device_id=device, device_id_type=MESH)

    def greet(i):
        device = (((xh + i // FEATS) % 2) * ZS + z, (fi + i) % FEATS)
        pl.semaphore_signal(barrier, inc=1, device_id=device, device_id_type=MESH)

    loop(1, 2 * FEATS, greet)
    pl.semaphore_wait(barrier, 2 * FEATS + 1)

    def swap_t(i):
        return remote(t_hbm.at[own_rows(i)], g.at[own_rows(i)], t_send.at[i], own_recv.at[i], partner)

    def swap_q(i):
        return remote(q_hbm.at[q_rows(i)], qb.at[1, q_rows(i)], away_send.at[i], away_recv.at[i], partner)

    def pass_q(i):
        return remote(qb.at[1, q_rows(i)], qb.at[1, q_rows(i)], fwd_send.at[i], away_recv.at[i], sibling)

    def share_q(i):
        return remote(q_hbm.at[q_rows(i)], qb.at[0, q_rows(i)], home_send.at[i], home_recv.at[i], sibling)

    def to_right(j, src):
        return remote(g.at[rows(src, CHUNK)], g.at[rows((j + 2) * PAIR, CHUNK)], r_send, r_recv.at[j], right)

    def to_left(j, src):
        return remote(g.at[rows(src, CHUNK)], g.at[rows((j + 2) * PAIR + CHUNK, CHUNK)], l_send, l_recv.at[j], left)

    def first_chunk(i):
        arrived(g.at[own_rows(i)], own_recv.at[i])
        to_right(i, i * CHUNK).start()
        to_left((i + 2) % 4, i * CHUNK).start()

    @pl.when(foreign)
    def _():
        for i in (0, 2, 1, 3):
            swap_t(i).start()

    @pl.when(native)
    def _():
        for i in (0, 2, 1, 3):
            first_chunk(i)

    share_e = remote(e_hbm, eb.at[c], e_send, e_recv, sibling)
    share_e.start()

    @pl.when(native)
    def _():
        def share(i):
            local_q(i).start()
            share_q(i).start()

        loop(0, QPARTS, share)

    layer = lax.broadcasted_iota(jnp.int32, (LAYERS, 128), 0)
    lane = lax.broadcasted_iota(jnp.int32, (LAYERS, 128), 1)
    low = jnp.zeros((LAYERS, 128), jnp.int32)
    high = jnp.zeros((LAYERS, 128), jnp.int32)
    for n in range(LAYERS):
        low = jnp.where(layer == n, offs[n], low)
        high = jnp.where(layer == n, offs[n + 1], high)

    def member(first):
        ids = lane + first
        return (ids >= low) & (ids < high)

    local_e.wait()

    def add_tile(i, acc):
        tile = eb[c, :, rows(i * 128, 128)]
        return acc + jnp.where(member(fi * WIDTH + i * 128), tile, 0.0)

    ls[fi] = lax.fori_loop(0, WIDTH // 128, add_tile, jnp.zeros((LAYERS, 128), jnp.float32))

    def share_sums(i):
        return remote(ls.at[fi], ls.at[fi], ls_send, ls_recv, (qi, (fi + i) % FEATS))

    loop(1, FEATS, lambda i: share_sums(i).start())

    @pl.when(foreign)
    def _():
        first_chunk(0)
        first_chunk(2)
        swap_q(0).start()
        first_chunk(1)
        swap_q(1).start()
        first_chunk(3)
        swap_q(2).start()
        swap_q(3).start()

    arrived(ls.at[pl.ds(0, FEATS - 1)], ls_recv)
    layer_sum = jnp.sum(jnp.sum(ls[...], axis=0), axis=1, keepdims=True)
    total = jnp.sum(layer_sum, axis=0, keepdims=True)
    counts = (high - low).astype(jnp.float32)
    damping = 0.05 * (layer_sum / counts + total / F)

    arrived(eb.at[1 - c], e_recv)
    first_feature = (xl * 8 + y * 2 + xh) * WIDTH

    def weigh(i):
        at = rows(i * 128, 128)
        damp = jnp.sum(jnp.where(member(first_feature + i * 128), damping, 0.0), axis=0, keepdims=True)
        wt[:, at] = 1.0 / (eb[xh, :, at] + damp)

    loop(0, WIDTH // 128, weigh)

    def send_scores(p, side, half, columns=pl.ds(0, QROWS)):
        late = p // 12
        distance = jnp.where(late > 0, 4 - p % 2, (p + 2) // 4)
        number = jnp.where(late > 0, p % 2 * 2 + (p - 12) // 2, (p + 2) % 4)
        source_z = (z + ZS + (2 * side - 1) * distance) % ZS
        part = jnp.where(p < 2, 2 * p + side, (number + 2 * side) % 4)
        mine = jnp.logical_and(half == 0, fi == c * 8 + source_z)
        src = pb.at[half, rows(p * PAIR + side * CHUNK, CHUNK), columns]
        dst = rb.at[slot, rows(part * CHUNK, CHUNK), columns]

        @pl.when(mine)
        def _():
            pltpu.make_async_copy(src, dst, o_recv.at[part]).start()

        @pl.when(jnp.logical_not(mine))
        def _():
            device = (((xh + half) % 2) * ZS + z, c * 8 + source_z)
            remote(src, dst, o_send, o_recv.at[part], device).start()

    def multiply(start, size, block):
        half, at, columns = block // 2, pl.ds(pl.multiple_of(start, PAIR), size), rows(block % 2 * 256, 256)
        scores = lax.dot_general(
            w[at, :], qb[half, columns, :], (((1,), (1,)), ((), ())), preferred_element_type=jnp.float32
        )
        pb[half, at, columns] = scores.astype(jnp.bfloat16)

    near = 1 - z % 2

    def order(n, turn):
        ring = jnp.where(n < 8, n - 2, jnp.where(n < turn, n - 6, jnp.where(n < 22, n - turn + 6, n - 12)))
        same = jnp.logical_or(n < 8, jnp.logical_and(n >= turn, n < 22))
        return jnp.where(n < 4, n // 2, ring), jnp.where(n < 4, n % 2, jnp.where(same, near, 1 - near))

    def backlog(groups, block):
        loop(0, groups, lambda b: multiply(b * (GROUP * PAIR), GROUP * PAIR, block))
        count = 2 * GROUP * groups

        def send(i):
            p, side = order((i + count // 4 * y) % count, 14 if groups == 2 else 16)
            send_scores(p, side, 1, pl.ds(block % 2 * 256, 256))

        loop(0, count, send)

    loop(0, QPARTS, lambda i: arrived(qb.at[0, q_rows(i)], home_recv.at[i]))

    def work(p):
        k = p - 2

        @pl.when(p >= 2)
        def _():
            arrived(g.at[rows(p * PAIR, CHUNK)], r_recv.at[k])
            arrived(g.at[rows(p * PAIR + CHUNK, CHUNK)], l_recv.at[k])

        def pass_on(j, pair):
            to_right(j, pair * PAIR).start()
            to_left(j, pair * PAIR + CHUNK).start()

        @pl.when(jnp.logical_and(p >= 2, p < 8))
        def _():
            pass_on(p + 2, p)

        @pl.when(jnp.logical_or(p == 10, p == 11))
        def _():
            pass_on(2 * p - 10, p)
            pass_on(2 * p - 9, p - 2)

        @pl.when(jnp.logical_and(foreign, jnp.logical_and(p >= 2, p < 6)))
        def _():
            swap_q(p - 2).wait_send()
            swap_q(p + 2).start()

        @pl.when(jnp.logical_and(foreign, jnp.logical_and(p >= 5, p < 13)))
        def _():
            arrived(qb.at[1, q_rows(p - 5)], away_recv.at[p - 5])
            pass_q(p - 5).start()

        def weight_rows(i):
            at = rows(i * 512, 512)
            raw = g[rows(p * PAIR, PAIR), at].astype(jnp.float32)
            w[rows(p * PAIR, PAIR), at] = (raw * wt[:, at]).astype(jnp.bfloat16)

        loop(0, WIDTH // 512, weight_rows)

        @pl.when(jnp.logical_and(native, p == SOME))
        def _():
            loop(0, QPARTS // 2, lambda i: arrived(qb.at[1, q_rows(i)], away_recv.at[i]))

        @pl.when(jnp.logical_and(native, p == BOTH))
        def _():
            loop(QPARTS // 2, QPARTS, lambda i: arrived(qb.at[1, q_rows(i)], away_recv.at[i]))

        def one_block(block):
            multiply(p * PAIR, PAIR, block)

            @pl.when(block % 2 == 1)
            def _():
                send_scores(p, 0, block // 2)
                send_scores(p, 1, block // 2)

            @pl.when(jnp.logical_and(block == 2, p < BOTH))
            def _():
                send_scores(p, 0, 1, pl.ds(0, 256))
                send_scores(p, 1, 1, pl.ds(0, 256))

        loop(0, 2 + p // SOME + p // BOTH, one_block)

        @pl.when(p == SOME)
        def _():
            backlog(SOME // GROUP, 2)

        @pl.when(p == BOTH)
        def _():
            backlog(BOTH // GROUP, 3)

    loop(0, PAIRS, work)

    for part in (0, 2, 1, 3):
        at = pl.ds(part * CHUNK, CHUNK)
        arrived(rb.at[:, at], o_recv.at[part])
        total = rb[0, at, :].astype(jnp.float32)
        for source in range(1, CHIPS):
            total += rb[source, at, :].astype(jnp.float32)
        out[at, :] = total

    sent = pl.ds(0, STEPS * CHUNK)
    arrived(g.at[sent], r_send)
    arrived(g.at[sent], l_send)
    arrived(pb.at[0], o_send)
    arrived(pb.at[1, pl.ds(0, (PAIRS - 2) * PAIR)], o_send)

    @pl.when(xl != c)
    def _():
        arrived(pb.at[1, pl.ds((PAIRS - 2) * PAIR, 2 * PAIR)], o_send)

    arrived(ls.at[pl.ds(0, FEATS - 1)], ls_send)
    share_e.wait_send()

    @pl.when(native)
    def _():
        loop(0, QPARTS, lambda i: share_q(i).wait_send())

    @pl.when(foreign)
    def _():
        loop(0, 4, lambda i: swap_t(i).wait_send())
        loop(4, QPARTS, lambda i: swap_q(i).wait_send())
        loop(0, QPARTS, lambda i: pass_q(i).wait_send())


def per_device(query_grads, train_grads, eigenvalues, offsets):
    dma = pltpu.SemaphoreType.DMA
    anywhere = pl.BlockSpec(memory_space=pl.ANY)
    return pl.pallas_call(
        kernel,
        out_shape=jax.ShapeDtypeStruct((ROWS, QROWS), jnp.float32),
        in_specs=[pl.BlockSpec(memory_space=pltpu.SMEM), anywhere, anywhere, anywhere],
        out_specs=pl.BlockSpec(memory_space=pltpu.VMEM),
        scratch_shapes=[
            pltpu.VMEM((PAIRS * PAIR, WIDTH), jnp.bfloat16),
            pltpu.VMEM((PAIRS * PAIR, WIDTH), jnp.bfloat16),
            pltpu.VMEM((2, QROWS, WIDTH), jnp.bfloat16),
            pltpu.VMEM((2, PAIRS * PAIR, QROWS), jnp.bfloat16),
            pltpu.VMEM((CHIPS, ROWS, QROWS), jnp.bfloat16),
            pltpu.VMEM((1, WIDTH), jnp.float32),
            pltpu.VMEM((2, 1, WIDTH), jnp.float32),
            pltpu.VMEM((FEATS, LAYERS, 128), jnp.float32),
            dma((4,)), dma((4,)),
            dma, dma((STEPS,)), dma, dma((STEPS,)),
            dma((QPARTS,)), dma((QPARTS,)), dma((QPARTS,)), dma((QPARTS,)), dma((QPARTS,)),
            dma, dma, dma,
            dma, dma,
            dma, dma((4,)),
        ],
        compiler_params=pltpu.CompilerParams(
            collective_id=0, has_side_effects=True, vmem_limit_bytes=56 * 2**20
        ),
        name="scores",
    )(offsets, query_grads, train_grads, eigenvalues.reshape(1, WIDTH))


def solution(mesh):
    return jax.shard_map(
        per_device,
        mesh=mesh,
        in_specs=(P("query", "feat"), P("query", "feat"), P("feat"), P()),
        out_specs=P("feat", "query"),
        check_vma=False,
    )
```

```python
import functools

import jax
import jax.numpy as jnp
from jax import lax
from jax.experimental import pallas as pl
from jax.experimental.pallas import tpu as pltpu
from jax.sharding import PartitionSpec as P

MESH = pl.DeviceIdType.MESH
F = 65536
LAYERS = 32
ZS = 8
FEATS = 16
CHIPS = 16
WIDTH = 4096
ROWS = 128
QROWS = 512
CHUNK = 32
PAIR = 2 * CHUNK
PAIRS = 16
STEPS = PAIRS - 2
QPARTS = 8
QCHUNK = QROWS // QPARTS
GROUP = 4
SOME = 8
BOTH = 12


def rows(start, size):
    return pl.ds(pl.multiple_of(start, size), size)


def kernel(
    offs, q_hbm, t_hbm, e_hbm, out,
    g, w, qb, pb, rb, wt, eb, ls,
    own_recv, t_send, r_send, r_recv, l_send, l_recv,
    home_recv, home_send, away_recv, away_send, fwd_send,
    e_copy, e_send, e_recv, ls_send, ls_recv, o_send, o_recv,
):
    qi, fi = lax.axis_index("query"), lax.axis_index("feat")
    xh, z = qi // ZS, qi % ZS
    xl, y, c = fi // 8, (fi // 2) % 4, fi % 2
    slot = (xh * 2 + xl) * 4 + y
    native = c == xh
    foreign = c != xh
    right = (xh * ZS + (z + 1) % ZS, fi)
    left = (xh * ZS + (z + ZS - 1) % ZS, fi)
    sibling = (qi, fi + 1 - 2 * c)
    partner = ((1 - xh) * ZS + z, fi + 1 - 2 * c)

    def remote(src, dst, send, recv, device):
        return pltpu.make_async_remote_copy(
            src_ref=src, dst_ref=dst, send_sem=send, recv_sem=recv, device_id=device, device_id_type=MESH
        )

    def arrived(ref, sem):
        pltpu.make_async_copy(ref, ref, sem).wait()

    def loop(low, high, body):
        def step(i, carry):
            body(i)
            return carry

        lax.fori_loop(low, high, step, 0)

    def own_rows(i):
        return rows(i * CHUNK, CHUNK)

    def q_rows(i):
        return rows(i * QCHUNK, QCHUNK)

    def local_t(i):
        return pltpu.make_async_copy(t_hbm.at[own_rows(i)], g.at[own_rows(i)], own_recv.at[i])

    def local_q(i):
        return pltpu.make_async_copy(q_hbm.at[q_rows(i)], qb.at[0, q_rows(i)], home_recv.at[i])

    local_e = pltpu.make_async_copy(e_hbm, eb.at[c], e_copy)
    local_e.start()

    @pl.when(native)
    def _():
        loop(0, 4, lambda i: local_t(i).start())

    barrier = pltpu.get_barrier_semaphore()
    for device in (left, right):
        pl.semaphore_signal(barrier, inc=1, device_id=device, device_id_type=MESH)

    def greet(i):
        device = (((xh + i // FEATS) % 2) * ZS + z, (fi + i) % FEATS)
        pl.semaphore_signal(barrier, inc=1, device_id=device, device_id_type=MESH)

    loop(1, 2 * FEATS, greet)
    pl.semaphore_wait(barrier, 2 * FEATS + 1)

    def swap_t(i):
        return remote(t_hbm.at[own_rows(i)], g.at[own_rows(i)], t_send.at[i], own_recv.at[i], partner)

    def swap_q(i):
        return remote(q_hbm.at[q_rows(i)], qb.at[1, q_rows(i)], away_send.at[i], away_recv.at[i], partner)

    def pass_q(i):
        return remote(qb.at[1, q_rows(i)], qb.at[1, q_rows(i)], fwd_send.at[i], away_recv.at[i], sibling)

    def share_q(i):
        return remote(q_hbm.at[q_rows(i)], qb.at[0, q_rows(i)], home_send.at[i], home_recv.at[i], sibling)

    def to_right(j, src):
        return remote(g.at[rows(src, CHUNK)], g.at[rows((j + 2) * PAIR, CHUNK)], r_send, r_recv.at[j], right)

    def to_left(j, src):
        return remote(g.at[rows(src, CHUNK)], g.at[rows((j + 2) * PAIR + CHUNK, CHUNK)], l_send, l_recv.at[j], left)

    def first_chunk(i):
        arrived(g.at[own_rows(i)], own_recv.at[i])
        to_right(i, i * CHUNK).start()
        to_left((i + 2) % 4, i * CHUNK).start()

    @pl.when(foreign)
    def _():
        for i in (0, 2, 1, 3):
            swap_t(i).start()

    @pl.when(native)
    def _():
        for i in (0, 2, 1, 3):
            first_chunk(i)

    share_e = remote(e_hbm, eb.at[c], e_send, e_recv, sibling)
    share_e.start()

    @pl.when(native)
    def _():
        def share(i):
            local_q(i).start()
            share_q(i).start()

        loop(0, QPARTS, share)

    layer = lax.broadcasted_iota(jnp.int32, (LAYERS, 128), 0)
    lane = lax.broadcasted_iota(jnp.int32, (LAYERS, 128), 1)
    low = jnp.zeros((LAYERS, 128), jnp.int32)
    high = jnp.zeros((LAYERS, 128), jnp.int32)
    for n in range(LAYERS):
        low = jnp.where(layer == n, offs[n], low)
        high = jnp.where(layer == n, offs[n + 1], high)

    def member(first):
        ids = lane + first
        return (ids >= low) & (ids < high)

    local_e.wait()

    def add_tile(i, acc):
        tile = eb[c, :, rows(i * 128, 128)]
        return acc + jnp.where(member(fi * WIDTH + i * 128), tile, 0.0)

    ls[fi] = lax.fori_loop(0, WIDTH // 128, add_tile, jnp.zeros((LAYERS, 128), jnp.float32))

    def share_sums(i):
        return remote(ls.at[fi], ls.at[fi], ls_send, ls_recv, (qi, (fi + i) % FEATS))

    loop(1, FEATS, lambda i: share_sums(i).start())

    @pl.when(foreign)
    def _():
        first_chunk(0)
        first_chunk(2)
        swap_q(0).start()
        first_chunk(1)
        swap_q(1).start()
        first_chunk(3)
        swap_q(2).start()
        swap_q(3).start()
        swap_q(4).start()

    arrived(ls.at[pl.ds(0, FEATS - 1)], ls_recv)
    layer_sum = jnp.sum(jnp.sum(ls[...], axis=0), axis=1, keepdims=True)
    total = jnp.sum(layer_sum, axis=0, keepdims=True)
    counts = (high - low).astype(jnp.float32)
    damping = 0.05 * (layer_sum / counts + total / F)

    arrived(eb.at[1 - c], e_recv)
    first_feature = (xl * 8 + y * 2 + xh) * WIDTH

    def weigh(i):
        at = rows(i * 128, 128)
        damp = jnp.sum(jnp.where(member(first_feature + i * 128), damping, 0.0), axis=0, keepdims=True)
        wt[:, at] = 1.0 / (eb[xh, :, at] + damp)

    loop(0, WIDTH // 128, weigh)

    def send_scores(p, side, half, columns=pl.ds(0, QROWS)):
        late = p // 12
        distance = jnp.where(late > 0, 4 - p % 2, (p + 2) // 4)
        number = jnp.where(late > 0, p % 2 * 2 + (p - 12) // 2, (p + 2) % 4)
        source_z = (z + ZS + (2 * side - 1) * distance) % ZS
        part = jnp.where(p < 2, 2 * p + side, (number + 2 * side) % 4)
        mine = jnp.logical_and(half == 0, fi == c * 8 + source_z)
        src = pb.at[half, rows(p * PAIR + side * CHUNK, CHUNK), columns]
        dst = rb.at[slot, rows(part * CHUNK, CHUNK), columns]

        @pl.when(mine)
        def _():
            pltpu.make_async_copy(src, dst, o_recv.at[part]).start()

        @pl.when(jnp.logical_not(mine))
        def _():
            device = (((xh + half) % 2) * ZS + z, c * 8 + source_z)
            remote(src, dst, o_send, o_recv.at[part], device).start()

    def multiply(start, size, block):
        half, at, columns = block // 2, pl.ds(pl.multiple_of(start, PAIR), size), rows(block % 2 * 256, 256)
        scores = lax.dot_general(
            w[at, :], qb[half, columns, :], (((1,), (1,)), ((), ())), preferred_element_type=jnp.float32
        )
        pb[half, at, columns] = scores.astype(jnp.bfloat16)

    near = 1 - z % 2

    def order(n, turn):
        ring = jnp.where(n < 8, n - 2, jnp.where(n < turn, n - 6, jnp.where(n < 22, n - turn + 6, n - 12)))
        same = jnp.logical_or(n < 8, jnp.logical_and(n >= turn, n < 22))
        return jnp.where(n < 4, n // 2, ring), jnp.where(n < 4, n % 2, jnp.where(same, near, 1 - near))

    def backlog(groups, block):
        loop(0, groups, lambda b: multiply(b * (GROUP * PAIR), GROUP * PAIR, block))
        count = 2 * GROUP * groups

        def send(i):
            p, side = order((i + count // 4 * y) % count, 14 if groups == 2 else 16)
            send_scores(p, side, 1, pl.ds(block % 2 * 256, 256))

        loop(0, count, send)

    loop(0, QPARTS, lambda i: arrived(qb.at[0, q_rows(i)], home_recv.at[i]))

    def work(p):
        k = p - 2

        @pl.when(p >= 2)
        def _():
            arrived(g.at[rows(p * PAIR, CHUNK)], r_recv.at[k])
            arrived(g.at[rows(p * PAIR + CHUNK, CHUNK)], l_recv.at[k])

        def pass_on(j, pair):
            to_right(j, pair * PAIR).start()
            to_left(j, pair * PAIR + CHUNK).start()

        @pl.when(jnp.logical_and(p >= 2, p < 8))
        def _():
            pass_on(p + 2, p)

        @pl.when(jnp.logical_or(p == 10, p == 11))
        def _():
            pass_on(2 * p - 10, p)
            pass_on(2 * p - 9, p - 2)

        @pl.when(jnp.logical_and(foreign, jnp.logical_and(p >= 2, p < 5)))
        def _():
            swap_q(p - 2).wait_send()
            swap_q(p + 3).start()

        @pl.when(jnp.logical_and(foreign, jnp.logical_and(p >= 5, p < 13)))
        def _():
            arrived(qb.at[1, q_rows(p - 5)], away_recv.at[p - 5])
            pass_q(p - 5).start()

        def weight_rows(i):
            at = rows(i * 512, 512)
            raw = g[rows(p * PAIR, PAIR), at].astype(jnp.float32)
            w[rows(p * PAIR, PAIR), at] = (raw * wt[:, at]).astype(jnp.bfloat16)

        loop(0, WIDTH // 512, weight_rows)

        @pl.when(jnp.logical_and(native, p == SOME))
        def _():
            loop(0, QPARTS // 2, lambda i: arrived(qb.at[1, q_rows(i)], away_recv.at[i]))

        @pl.when(jnp.logical_and(native, p == BOTH))
        def _():
            loop(QPARTS // 2, QPARTS, lambda i: arrived(qb.at[1, q_rows(i)], away_recv.at[i]))

        def one_block(block):
            multiply(p * PAIR, PAIR, block)

            @pl.when(block % 2 == 1)
            def _():
                send_scores(p, 0, block // 2)
                send_scores(p, 1, block // 2)

            @pl.when(jnp.logical_and(block == 2, p < BOTH))
            def _():
                send_scores(p, 0, 1, pl.ds(0, 256))
                send_scores(p, 1, 1, pl.ds(0, 256))

        loop(0, 2 + p // SOME + p // BOTH, one_block)

        @pl.when(p == SOME)
        def _():
            backlog(SOME // GROUP, 2)

        @pl.when(p == BOTH)
        def _():
            backlog(BOTH // GROUP, 3)

    loop(0, PAIRS, work)

    for part in (0, 2, 1, 3):
        at = pl.ds(part * CHUNK, CHUNK)
        arrived(rb.at[:, at], o_recv.at[part])
        total = rb[0, at, :].astype(jnp.float32)
        for source in range(1, CHIPS):
            total += rb[source, at, :].astype(jnp.float32)
        out[at, :] = total

    sent = pl.ds(0, STEPS * CHUNK)
    arrived(g.at[sent], r_send)
    arrived(g.at[sent], l_send)
    arrived(pb.at[0], o_send)
    arrived(pb.at[1, pl.ds(0, (PAIRS - 2) * PAIR)], o_send)

    @pl.when(xl != c)
    def _():
        arrived(pb.at[1, pl.ds((PAIRS - 2) * PAIR, 2 * PAIR)], o_send)

    arrived(ls.at[pl.ds(0, FEATS - 1)], ls_send)
    share_e.wait_send()

    @pl.when(native)
    def _():
        loop(0, QPARTS, lambda i: share_q(i).wait_send())

    @pl.when(foreign)
    def _():
        loop(0, 4, lambda i: swap_t(i).wait_send())
        loop(3, QPARTS, lambda i: swap_q(i).wait_send())
        loop(0, QPARTS, lambda i: pass_q(i).wait_send())


def per_device(query_grads, train_grads, eigenvalues, offsets):
    dma = pltpu.SemaphoreType.DMA
    anywhere = pl.BlockSpec(memory_space=pl.ANY)
    return pl.pallas_call(
        kernel,
        out_shape=jax.ShapeDtypeStruct((ROWS, QROWS), jnp.float32),
        in_specs=[pl.BlockSpec(memory_space=pltpu.SMEM), anywhere, anywhere, anywhere],
        out_specs=pl.BlockSpec(memory_space=pltpu.VMEM),
        scratch_shapes=[
            pltpu.VMEM((PAIRS * PAIR, WIDTH), jnp.bfloat16),
            pltpu.VMEM((PAIRS * PAIR, WIDTH), jnp.bfloat16),
            pltpu.VMEM((2, QROWS, WIDTH), jnp.bfloat16),
            pltpu.VMEM((2, PAIRS * PAIR, QROWS), jnp.bfloat16),
            pltpu.VMEM((CHIPS, ROWS, QROWS), jnp.bfloat16),
            pltpu.VMEM((1, WIDTH), jnp.float32),
            pltpu.VMEM((2, 1, WIDTH), jnp.float32),
            pltpu.VMEM((FEATS, LAYERS, 128), jnp.float32),
            dma((4,)), dma((4,)),
            dma, dma((STEPS,)), dma, dma((STEPS,)),
            dma((QPARTS,)), dma((QPARTS,)), dma((QPARTS,)), dma((QPARTS,)), dma((QPARTS,)),
            dma, dma, dma,
            dma, dma,
            dma, dma((4,)),
        ],
        compiler_params=pltpu.CompilerParams(
            collective_id=0, has_side_effects=True, vmem_limit_bytes=56 * 2**20
        ),
        name="scores",
    )(offsets, query_grads, train_grads, eigenvalues.reshape(1, WIDTH))


def solution(mesh):
    return jax.shard_map(
        per_device,
        mesh=mesh,
        in_specs=(P("query", "feat"), P("query", "feat"), P("feat"), P()),
        out_specs=P("feat", "query"),
        check_vma=False,
    )
```
